128 devices in a mesh: outer: 4 (over x_hi, core), inner: 32 (over z, x_lo, y).
Axes of the slice: x: 4 (x_hi: 2, x_lo: 2; x = x_hi * 2 + x_lo), y: 4, z: 4, core: 2. Of those that a mesh axis runs over, the one named last changes fastest.
Arguments:
- coeffs: bfloat16 [32, 8, 131072], P(None, None, ('outer', 'inner')), may hold values from -6 to 6
- source_mats: bfloat16 [2, 2, 32, 32, 131072], P(None, None, None, None, ('outer', 'inner')), may hold values from -0.75 to 0.75
- middle_mats: bfloat16 [32, 32, 131072], P(None, None, ('outer', 'inner')), may hold values from -1 to 1
- target_mats: bfloat16 [2, 2, 32, 32, 131072], P(None, None, None, None, ('outer', 'inner')), may hold values from -0.75 to 0.75
Outputs:
- target_coeffs: bfloat16 [32, 8, 131072], P(None, None, ('outer', 'inner'))
The draws below stay inside these ranges and needn't reach their ends.
All inputs are finite; a program needn't handle non-finite values.
Results may differ from the reference program's by a relative error of at most 0.0071.
Values may be sent and summed in bfloat16 or wider, within the bound.
A program may use at most 192 MiB of HBM per device.

```python
import jax
import jax.numpy as jnp

R = 32
P_SIZE = 8
BOX_DEV = 1024
BOXES = 131072
SLAB = 32
N_OUTER = 4
N_INNER = 32


def steps_of(key, dims, split, least, largest):
    factor_of = 1.0
    for dim, blocks in split:
        draws = jax.random.uniform(jax.random.fold_in(jax.random.fold_in(key, 6), dim), (blocks,), jnp.float32, least / len(split), largest / len(split))
        factor_of = factor_of * jnp.repeat(jnp.exp(draws), dims[dim] // blocks).reshape((-1,) + (1,) * (len(dims) - 1 - dim))
    return factor_of


def centred(own_key, dims, scale, bound, split=(), dtype=jnp.bfloat16):
    level = steps_of(own_key, dims, split, -0.22, 0.18) if split else 1.0
    values = jax.random.normal(own_key, dims, jnp.float32) * scale * level
    return jnp.minimum(jnp.maximum(values, -bound), bound).astype(dtype)


def setup_inputs(seed: int = 0) -> dict:
    key_of = jax.random.split(jax.random.key(seed), 5)
    coeffs = centred(key_of[0], (R, P_SIZE, BOXES), 1.0, 6.0, ((2, 128),))
    source_mats = centred(key_of[1], (2, 2, R, R, BOXES), (2 * R) ** -0.5, 0.75, ((4, 128),))
    middle_mats = centred(key_of[2], (R, R, BOXES), R ** -0.5, 1.0, ((2, 128),))
    target_mats = centred(key_of[3], (2, 2, R, R, BOXES), (2 * R) ** -0.5, 0.75, ((4, 128),))
    return dict(coeffs=coeffs, source_mats=source_mats, middle_mats=middle_mats, target_mats=target_mats)


def partner(x, stride):
    rows, probes, boxes = x.shape
    folded = x.reshape(rows, probes, boxes // (2 * stride), 2, stride)
    return jnp.flip(folded, 3).reshape(rows, probes, boxes)


def apply_box(mats, x):
    return jnp.einsum("ijb,jpb->ipb", mats.astype(jnp.float32), x.astype(jnp.float32))


def level(mats, x, stride):
    total = apply_box(mats[0], x) + apply_box(mats[1], partner(x, stride))
    return total.astype(jnp.bfloat16)


def reference(coeffs, source_mats, middle_mats, target_mats):
    x = coeffs
    for step in range(2):
        x = level(source_mats[step], x, (BOX_DEV * N_INNER) * (2 ** step))
    x = apply_box(middle_mats, x).astype(jnp.bfloat16)
    x = x.reshape(R, P_SIZE, N_OUTER, N_INNER, N_INNER, SLAB)
    x = jnp.swapaxes(x, 3, 4).reshape(R, P_SIZE, BOXES)
    for step in range(2):
        x = level(target_mats[step], x, BOX_DEV * (2 ** step))
    return x
```

```python
import jax
import jax.numpy as jnp
from jax import lax
from jax.experimental import pallas as pl
from jax.experimental.pallas import tpu as pltpu
from jax.sharding import PartitionSpec as P

F32 = jnp.float32
BF16 = jnp.bfloat16
MESH = pl.DeviceIdType.MESH
CHUNKS = 4
CHUNK = (8, 4, 16, 128)


def flip1(v):
    return v + 1 - 2 * lax.rem(v, 2)


def flip(v, k):
    low = lax.rem(v + k, 2)
    high = lax.rem(lax.div(v, 2) + lax.div(k, 2), 2)
    return high * 2 + low


def pattern(per, cols):
    r = lax.broadcasted_iota(jnp.int32, (16, cols), 0)
    k = lax.broadcasted_iota(jnp.int32, (16, cols), 1)
    shift = per.bit_length() - 1
    return (((k >> shift) & 7) + ((k >> 3) & 1) * 8 == r).astype(BF16)


def level(mats, xs, store):
    n = len(mats)

    def body(ro, _):
        pat = pattern(64 * n, 512 * n)
        for p in range(0, 8, 2):
            halves = []
            for q in (p, p + 1):
                x = [[xs[s][q, rt] for rt in range(4)] for s in range(n)]
                halves.append(
                    jnp.concatenate(
                        [
                            mats[s](ro * 8 + i, rt) * x[s][rt]
                            for i in range(8)
                            for s in range(n)
                            for rt in range(4)
                        ],
                        0,
                    )
                )
            y = jnp.dot(pat, jnp.concatenate(halves, 1), preferred_element_type=F32)
            store(ro, p, y[:, :128])
            store(ro, p + 1, y[:, 128:])
        return 0

    lax.fori_loop(0, 4, body, 0)


def level_out(mats, xs, store):
    n = len(mats)

    def body(ro, _):
        pat = pattern(64 * n, 512 * n)
        for h in range(0, 8, 2):
            halves = []
            for i in (ro * 8 + h, ro * 8 + h + 1):
                m = [[mats[s](i, rt) for rt in range(4)] for s in range(n)]
                halves.append(
                    jnp.concatenate(
                        [
                            m[s][rt] * xs[s][p, rt]
                            for p in range(8)
                            for s in range(n)
                            for rt in range(4)
                        ],
                        0,
                    )
                )
            y = jnp.dot(pat, jnp.concatenate(halves, 1), preferred_element_type=F32)
            store(ro * 8 + h, y[:, :128])
            store(ro * 8 + h + 1, y[:, 128:])
        return 0

    lax.fori_loop(0, 4, body, 0)


def lane_blocks(v):
    lane = lax.broadcasted_iota(jnp.int32, (16, 128), 1)
    low = lane < 64
    even = (lane & 32) == 0
    s = [None] * 4
    for a in range(2):
        s[a] = jnp.where(low, v[a], pltpu.roll(v[a + 2], 64, 1))
        s[a + 2] = jnp.where(low, pltpu.roll(v[a], 64, 1), v[a + 2])
    out = [None] * 4
    for a in (0, 2):
        out[a] = jnp.where(even, s[a], pltpu.roll(s[a + 1], 32, 1))
        out[a + 1] = jnp.where(even, pltpu.roll(s[a], 96, 1), s[a + 1])
    return out


def kernel(
    coeffs, source, middle, target, out,
    ms, mm, mt, c0, x0, x1, x1p, x2, tr, snd, rcv, pk, un, x3, x4, x4p, res,
    m_sem, c_sem, cs_sem, cr_sem, xs_sem, xr_sem, as_sem, ar_sem, al_sem,
    ys_sem, yr_sem, yl_sem, ts_sem, trr_sem, o_sem,
):
    outer, inner = lax.axis_index("outer"), lax.axis_index("inner")
    z, xl, y = lax.div(inner, 8), lax.rem(lax.div(inner, 4), 2), lax.rem(inner, 4)
    core_dev = (flip1(outer), inner)
    far_dev = (lax.rem(outer + 2, 4), inner)

    def zx_dev(zt, xt):
        return (outer, zt * 8 + xt * 4 + y)

    def y_dev(yt):
        return (outer, inner - y + yt)

    def order(k):
        return flip(z, k)

    def rows(k):
        return pl.ds(pl.multiple_of(order(k) * 16, 16), 16)

    def mat_copy(stage, k):
        r = rows(k)
        if stage < 2:
            pair = (source.at[stage, :, :, :, r], ms.at[stage, :, :, :, r])
        elif stage == 2:
            pair = (middle.at[:, :, r], mm.at[:, :, r])
        else:
            pair = (target.at[stage - 3, :, :, :, r], mt.at[stage - 3, :, :, :, r])
        return pltpu.make_async_copy(*pair, m_sem.at[stage, k])

    def coeff_copy(k):
        return pltpu.make_async_copy(coeffs.at[:, rows(k)], c0.at[0, :, rows(k)], c_sem.at[k])

    def remote(src, dst, send, recv, device):
        return pltpu.make_async_remote_copy(
            src_ref=src, dst_ref=dst, send_sem=send, recv_sem=recv, device_id=device, device_id_type=MESH
        )

    def coeff_send(k):
        return remote(coeffs.at[:, rows(k)], c0.at[1, :, rows(k)], cs_sem.at[k], cr_sem.at[k], core_dev)

    def far_send(k):
        return remote(x1.at[k], x1p.at[k], xs_sem.at[k], xr_sem.at[k], far_dev)

    def swap_send(k, xt):
        return remote(
            snd.at[k, xt], rcv.at[k, xl], as_sem.at[k, xt], ar_sem.at[k, xl], zx_dev(order(k), xt)
        )

    def swap_arrival(k, xt):
        return remote(
            snd.at[k, xt], rcv.at[k, xt], as_sem.at[k, xt], ar_sem.at[k, xt], zx_dev(order(k), xt)
        )

    def swap_local():
        return pltpu.make_async_copy(snd.at[0, xl], rcv.at[0, xl], al_sem)

    def y_send(k, d):
        yt = flip(y, d)
        return remote(pk.at[k, lax.div(yt, 2)], un.at[k, y], ys_sem.at[k, d], yr_sem.at[k, d], y_dev(yt))

    def y_arrival(k, d):
        yt = flip(y, d)
        return remote(pk.at[k, lax.div(yt, 2)], un.at[k, yt], ys_sem.at[k, d], yr_sem.at[k, d], y_dev(yt))

    def y_local(k):
        return pltpu.make_async_copy(pk.at[k, lax.div(y, 2)], un.at[k, y], yl_sem.at[k])

    def last_send(k):
        return remote(x4.at[k], x4p.at[k], ts_sem.at[k], trr_sem.at[k], y_dev(flip(y, 2)))

    def out_copy(k):
        return pltpu.make_async_copy(res.at[:, rows(k)], out.at[:, rows(k)], o_sem.at[k])

    def each(fn):
        def body(k, _):
            fn(k)
            return 0

        lax.fori_loop(0, CHUNKS, body, 0)

    each(lambda k: coeff_copy(k).start())
    for stage in range(5):
        each(lambda k, stage=stage: mat_copy(stage, k).start())

    barrier = pltpu.get_barrier_semaphore()
    peers = [core_dev, far_dev] + [y_dev(flip(y, d)) for d in (1, 2, 3)]
    peers += [zx_dev(flip(z, k), x) for k in range(4) for x in ((flip1(xl),) if k == 0 else (0, 1))]
    for peer in peers:
        pl.semaphore_signal(barrier, inc=1, device_id=peer, device_id_type=MESH)
    pl.semaphore_wait(barrier, len(peers))

    each(lambda k: coeff_send(k).start())

    def mats(ref, stage, k, count):
        r = rows(k)
        if ref is mm:
            return [lambda i, rt: mm[i, rt, r, :]]
        return [lambda i, rt, s=s: ref[stage, s, i, rt, r, :] for s in range(count)]

    def first_level(k, _):
        coeff_copy(k).wait()
        coeff_send(k).wait_recv()
        m = lax.broadcasted_iota(jnp.int32, (128, 128), 0)
        c = lax.broadcasted_iota(jnp.int32, (128, 128), 1)
        perm = (((c & 7) * 16 + ((c >> 3) & 1) * 8 + (c >> 4)) == m).astype(BF16)
        for rt in range(4):
            w = jnp.concatenate(
                [
                    jnp.concatenate([c0[s, rt * 8 + j, rows(k), :] for j in range(8)], 0)
                    for s in range(2)
                ],
                1,
            )
            v = jnp.dot(perm, w, preferred_element_type=F32).astype(BF16)
            for s in range(2):
                for p in range(8):
                    x0[s, p, rt] = v[p * 16 : p * 16 + 16, s * 128 : s * 128 + 128]
        mat_copy(0, k).wait()

        def store(ro, p, v):
            x1[k, p, ro] = v.astype(BF16)

        level(mats(ms, 0, k, 2), [x0.at[0], x0.at[1]], store)
        far_send(k).start()
        return 0

    lax.fori_loop(0, CHUNKS, first_level, 0)

    def second_level(k):
        far_send(k).wait_recv()
        mat_copy(1, k).wait()

        def store2(ro, p, v):
            x2[p, ro] = v.astype(BF16)

        level(mats(ms, 1, k, 2), [x1.at[k], x1p.at[k]], store2)
        mat_copy(2, k).wait()

        def store_mid(ro, p, v):
            tr[p, ro] = v

        level(mats(mm, 0, k, 1), [x2], store_mid)
        for p in range(8):
            for lt in range(2):
                for pair in range(2):
                    snd[k, lt, p, pair] = jnp.concatenate(
                        [tr[p, pair * 2 + h, lt * 8 : lt * 8 + 8, :] for h in range(2)], 0
                    ).astype(BF16)

        @pl.when(k == 0)
        def _():
            swap_local().start()
            swap_send(0, flip1(xl)).start()

        @pl.when(k > 0)
        def _():
            for xt in range(2):
                swap_send(k, xt).start()

    def regroup(k):
        @pl.when(k == 0)
        def _():
            swap_local().wait()
            swap_arrival(0, flip1(xl)).wait_recv()

        @pl.when(k > 0)
        def _():
            for xt in range(2):
                swap_arrival(k, xt).wait_recv()

        for p in range(8):
            v = lane_blocks([rcv[k, lt, p, pair].astype(F32) for lt in range(2) for pair in range(2)])
            for b in range(4):
                pk[k, b // 2, b % 2, p] = v[b].astype(BF16)
        y_local(k).start()
        for d in (1, 2, 3):
            y_send(k, d).start()

    def third_level(k):
        y_local(k).wait()
        for d in (1, 2, 3):
            y_arrival(k, d).wait_recv()
        for s in range(2):
            which = lax.rem(y, 2) if s == 0 else 1 - lax.rem(y, 2)
            for p in range(8):
                v = lane_blocks([un[k, b, which, p].astype(F32) for b in range(4)])
                for pair in range(2):
                    for h in range(2):
                        x3[s, p, pair * 2 + h] = jnp.concatenate(
                            [v[lt * 2 + pair][h * 8 : h * 8 + 8] for lt in range(2)], 0
                        ).astype(BF16)
        mat_copy(3, k).wait()

        def store(ro, p, v):
            x4[k, p, ro] = v.astype(BF16)

        level(mats(mt, 0, k, 2), [x3.at[0], x3.at[1]], store)
        last_send(k).start()

    def fourth_level(k):
        last_send(k).wait_recv()
        mat_copy(4, k).wait()

        def store(i, v):
            res[i, rows(k), :] = v.astype(BF16)

        level_out(mats(mt, 1, k, 2), [x4.at[k], x4p.at[k]], store)
        out_copy(k).start()

    stages = (second_level, regroup, third_level, fourth_level)

    def step(n, _):
        for late, stage in enumerate(stages):

            @pl.when(jnp.logical_and(n >= late, n < CHUNKS + late))
            def _(late=late, stage=stage):
                stage(n - late)

        return 0

    lax.fori_loop(0, CHUNKS + len(stages) - 1, step, 0)

    def finish(k):
        out_copy(k).wait()
        coeff_send(k).wait_send()
        far_send(k).wait_send()
        for d in (1, 2, 3):
            y_send(k, d).wait_send()
        last_send(k).wait_send()

        @pl.when(k == 0)
        def _():
            swap_send(0, flip1(xl)).wait_send()

        @pl.when(k > 0)
        def _():
            for xt in range(2):
                swap_send(k, xt).wait_send()

    each(finish)


def lane_tiles(a):
    lead, rows = a.shape[:-2], a.shape[-2]
    d = len(lead)
    a = a.reshape(*lead, rows // 8, 8, 8, 128)
    a = a.transpose(*range(d + 1), d + 2, d + 1, d + 3)
    return a.reshape(*lead, rows // 8, 64, 128)


def per_device(coeffs, source_mats, middle_mats, target_mats):
    hbm = pl.BlockSpec(memory_space=pl.ANY)
    vm = lambda *s: pltpu.VMEM(s, BF16)
    dma = lambda *s: pltpu.SemaphoreType.DMA(s)
    out = pl.pallas_call(
        kernel,
        out_shape=jax.ShapeDtypeStruct((32, 64, 128), BF16),
        in_specs=[hbm] * 4,
        out_specs=hbm,
        scratch_shapes=[
            vm(2, 2, 32, 4, 64, 128),
            vm(32, 4, 64, 128),
            vm(2, 2, 32, 4, 64, 128),
            vm(2, 32, 64, 128),
            vm(2, *CHUNK),
            vm(4, *CHUNK),
            vm(4, *CHUNK),
            vm(*CHUNK),
            pltpu.VMEM(CHUNK, F32),
            vm(4, 2, 8, 2, 16, 128),
            vm(4, 2, 8, 2, 16, 128),
            vm(4, 2, 2, 8, 16, 128),
            vm(4, 4, 2, 8, 16, 128),
            vm(2, *CHUNK),
            vm(4, *CHUNK),
            vm(4, *CHUNK),
            vm(32, 64, 128),
            dma(5, 4), dma(4), dma(4), dma(4), dma(4), dma(4), dma(4, 2), dma(4, 2),
            pltpu.SemaphoreType.DMA,
            dma(4, 4), dma(4, 4), dma(4), dma(4), dma(4), dma(4),
        ],
        compiler_params=pltpu.CompilerParams(
            collective_id=0, has_side_effects=True, vmem_limit_bytes=60 << 20
        ),
        name="butterfly",
    )(
        lane_tiles(coeffs).reshape(32, 64, 128),
        lane_tiles(source_mats),
        lane_tiles(middle_mats),
        lane_tiles(target_mats),
    )
    return out.reshape(32, 8, 8, 128).swapaxes(1, 2).reshape(32, 8, 1024)


def solution(mesh):
    return jax.shard_map(
        per_device,
        mesh=mesh,
        in_specs=(
            P(None, None, ("outer", "inner")),
            P(None, None, None, None, ("outer", "inner")),
            P(None, None, ("outer", "inner")),
            P(None, None, None, None, ("outer", "inner")),
        ),
        out_specs=P(None, None, ("outer", "inner")),
        check_vma=False,
    )
```

```python
import jax
import jax.numpy as jnp
from jax import lax
from jax.experimental import pallas as pl
from jax.experimental.pallas import tpu as pltpu
from jax.sharding import PartitionSpec as P

F32 = jnp.float32
BF16 = jnp.bfloat16
MESH = pl.DeviceIdType.MESH
TILES = 8
EARLY = 4
LAGS = (0, 0, 4, 6, 8, 9, 10)
PAIRS = 4
TILE = (16, 16, 128)


def flip1(v):
    return v + 1 - 2 * lax.rem(v, 2)


def flip(v, k):
    total = 0
    for bit in (1, 2, 4):
        total = total + bit * lax.rem(lax.div(v, bit) + lax.div(k, bit), 2)
    return total


def lane_blocks(v):
    lane = lax.broadcasted_iota(jnp.int32, (16, 128), 1)
    low = lane < 64
    even = (lane & 32) == 0
    s = [None] * 4
    for a in range(2):
        s[a] = jnp.where(low, v[a], pltpu.roll(v[a + 2], 64, 1))
        s[a + 2] = jnp.where(low, pltpu.roll(v[a], 64, 1), v[a + 2])
    out = [None] * 4
    for a in (0, 2):
        out[a] = jnp.where(even, s[a], pltpu.roll(s[a + 1], 32, 1))
        out[a + 1] = jnp.where(even, pltpu.roll(s[a], 96, 1), s[a + 1])
    return out


def level(mats, xf, mf, emit, part=None):
    n = len(mats)

    def widen(g, slot):
        for s in range(n):
            mf[slot, s] = mats[s](g * 4).astype(F32)

    widen(0, 0)

    def body(h, _):
        for slot in range(2):
            g = h * 2 + slot
            widen(lax.rem(g + 1, 8), 1 - slot)
            acc = [None if part is None else part[g * 4 + i] for i in range(4)]
            for s in range(n):
                for j in range(32):
                    x = xf[s, j]
                    for i in range(4):
                        v = x * mf[slot, s, i, j : j + 1, :]
                        acc[i] = v if acc[i] is None else acc[i] + v
            emit(g * 4, acc)
        return 0

    lax.fori_loop(0, 4, body, 0)


def kernel(
    coeffs, source, middle, target, out,
    ms, mm, mt, c0, x1, x1p, snd, rcv, pk, un, x4, x4p, res, xf, mf, part, fin,
    m_sem, c_sem, cs_sem, cr_sem, xs_sem, xr_sem, as_sem, ar_sem, al_sem,
    ys_sem, yr_sem, yl_sem, ts_sem, tr_sem, o_sem,
):
    outer, inner = lax.axis_index("outer"), lax.axis_index("inner")
    own, y = lax.div(inner, 4), lax.rem(inner, 4)
    core_dev = (flip1(outer), inner)
    far_dev = (lax.rem(outer + 2, 4), inner)

    def ring_dev(k):
        return (outer, flip(own, k) * 4 + y)

    def y_dev(d):
        return (outer, own * 4 + flip(y, d))

    def tile(k):
        return flip(own, k)

    def lanes(k):
        return pl.ds(pl.multiple_of(tile(k) * 128, 128), 128)

    def pair(q):
        return flip(lax.div(own, 2), q)

    def pair_lanes(q):
        return pl.ds(pl.multiple_of(pair(q) * 256, 256), 256)

    def pair_rows(q):
        return pl.ds(pl.multiple_of(pair(q) * 16, 16), 16)

    def mat_copy(stage, q):
        r = pair_lanes(q)
        if stage < 4:
            at = (stage // 2, stage % 2, slice(None), slice(None), r)
            ends = (source.at[at], ms.at[at])
        elif stage == 4:
            ends = (middle.at[:, :, r], mm.at[:, :, r])
        else:
            at = ((stage - 5) // 2, (stage - 5) % 2, slice(None), slice(None), r)
            ends = (target.at[at], mt.at[at])
        return pltpu.make_async_copy(*ends, m_sem.at[stage, q])

    def coeff_copy(q):
        return pltpu.make_async_copy(coeffs.at[:, pair_rows(q)], c0.at[0, :, pair_rows(q)], c_sem.at[q])

    def remote(src, dst, send, recv, device):
        return pltpu.make_async_remote_copy(
            src_ref=src, dst_ref=dst, send_sem=send, recv_sem=recv, device_id=device, device_id_type=MESH
        )

    def coeff_send(q):
        return remote(coeffs.at[:, pair_rows(q)], c0.at[1, :, pair_rows(q)], cs_sem.at[q], cr_sem.at[q], core_dev)

    def far_send(k):
        return remote(x1.at[k], x1p.at[k], xs_sem.at[k], xr_sem.at[k], far_dev)

    def swap_send(k):
        return remote(snd.at[k], rcv.at[k], as_sem.at[k], ar_sem.at[k], ring_dev(k))

    def swap_local():
        return pltpu.make_async_copy(snd.at[0], rcv.at[0], al_sem)

    def y_send(k, d):
        return remote(
            pk.at[k, lax.div(flip(y, d), 2)], un.at[k, y], ys_sem.at[k, d], yr_sem.at[k, d], y_dev(d)
        )

    def y_arrival(k, d):
        return remote(
            pk.at[k, lax.div(flip(y, d), 2)], un.at[k, flip(y, d)], ys_sem.at[k, d], yr_sem.at[k, d], y_dev(d)
        )

    def y_local(k):
        return pltpu.make_async_copy(pk.at[k, lax.div(y, 2)], un.at[k, y], yl_sem.at[k])

    def last_send(k):
        return remote(x4.at[k], x4p.at[k], ts_sem.at[k], tr_sem.at[k], y_dev(2))

    def out_copy(q):
        return pltpu.make_async_copy(res.at[:, pair_rows(q)], out.at[:, pair_rows(q)], o_sem.at[q])

    def each(count, fn):
        def body(k, _):
            fn(k)
            return 0

        lax.fori_loop(0, count, body, 0)

    barrier = pltpu.get_barrier_semaphore()
    peers = [core_dev, far_dev] + [y_dev(d) for d in (1, 2, 3)] + [ring_dev(k) for k in range(1, 8)]
    for peer in peers:
        pl.semaphore_signal(barrier, inc=1, device_id=peer, device_id_type=MESH)

    def start_pair(q):
        coeff_copy(q).start()
        mat_copy(0, q).start()

    each(PAIRS, start_pair)
    for stage in range(1, 9):
        each(PAIRS, lambda q, stage=stage: mat_copy(stage, q).start())

    def await_pair(k, *waits):
        @pl.when(lax.rem(k, 2) == 0)
        def _():
            for wait in waits:
                wait(lax.div(k, 2))

    def mats(ref, lead, k):
        ln = lanes(k)
        return [lambda i, at=at: ref[(*at, pl.ds(i, 4), slice(None), ln)] for at in lead]

    def fill(s, ref):
        for h in range(16):
            v = ref[h].astype(F32)
            xf[s, 2 * h] = v[:8]
            xf[s, 2 * h + 1] = v[8:]

    def emit_to(ref):
        def emit(i, acc):
            h = lax.div(i, 2)
            for a in range(2):
                ref[h + a] = jnp.concatenate(acc[2 * a : 2 * a + 2], 0).astype(BF16)

        return emit

    def keep(ref):
        def emit(i, acc):
            for a in range(4):
                ref[i + a] = acc[a]

        return emit

    def first_fill(s, k):
        upper = lax.rem(tile(k), 2) == 1
        rows = pair_rows(lax.div(k, 2))
        for j in range(32):
            v = c0[s, j, rows, :].astype(F32)
            xf[0, j] = jnp.where(upper, v[8:], v[:8])

    def first_own(k):
        await_pair(k, lambda q: coeff_copy(q).wait(), lambda q: mat_copy(0, q).wait())
        first_fill(0, k)
        level(mats(ms, ((0, 0),), k), xf, mf, keep(part.at[k]))

    def first_level(k):
        await_pair(k, lambda q: coeff_send(q).wait_recv(), lambda q: mat_copy(1, q).wait())
        first_fill(1, k)
        level(mats(ms, ((0, 1),), k), xf, mf, emit_to(x1.at[k]), part.at[k])
        far_send(k).start()

    def second_own(k):
        await_pair(k, lambda q: mat_copy(2, q).wait())
        fill(0, x1.at[k])
        level(mats(ms, ((1, 0),), k), xf, mf, keep(part.at[k]))

    def second_level(k):
        await_pair(k, lambda q: mat_copy(3, q).wait(), lambda q: mat_copy(4, q).wait())
        far_send(k).wait_recv()
        fill(0, x1p.at[k])

        def emit(i, acc):
            for a in range(4):
                xf[1, i + a] = acc[a].astype(BF16).astype(F32)

        level(mats(ms, ((1, 1),), k), xf, mf, emit, part.at[k])
        level(mats(mm, ((),), k), xf.at[1:2], mf, emit_to(snd.at[k]))

        @pl.when(k == 0)
        def _():
            swap_local().start()

        @pl.when(k > 0)
        def _():
            swap_send(k).start()

    def regroup(k):
        @pl.when(k == 0)
        def _():
            swap_local().wait()

        @pl.when(k > 0)
        def _():
            swap_send(k).wait_recv()

        for a in range(4):
            v = lane_blocks([rcv[k, a * 4 + c].astype(F32) for c in range(4)])
            for b in range(4):
                pk[k, b // 2, b % 2, a] = v[b].astype(BF16)
        for d in (1, 2, 3):
            y_send(k, d).start()
        y_local(k).start()

    def third_level(k):
        await_pair(k, lambda q: mat_copy(5, q).wait(), lambda q: mat_copy(6, q).wait())
        y_local(k).wait()
        for d in (1, 2, 3):
            y_arrival(k, d).wait_recv()
        for s in range(2):
            which = lax.rem(y, 2) if s == 0 else 1 - lax.rem(y, 2)
            for a in range(4):
                v = lane_blocks([un[k, b, which, a].astype(F32) for b in range(4)])
                for c in range(4):
                    xf[s, a * 8 + c * 2] = v[c][:8]
                    xf[s, a * 8 + c * 2 + 1] = v[c][8:]
        level(mats(mt, ((0, 0), (0, 1)), k), xf, mf, emit_to(x4.at[k]))
        last_send(k).start()

    def fourth_own(k):
        await_pair(k, lambda q: mat_copy(7, q).wait())
        fill(0, x4.at[k])
        level(mats(mt, ((1, 0),), k), xf, mf, keep(part.at[k]))

    def fourth_level(k):
        await_pair(k, lambda q: mat_copy(8, q).wait())
        last_send(k).wait_recv()
        fill(0, x4p.at[k])
        half = lax.rem(tile(k), 2)
        level(mats(mt, ((1, 1),), k), xf, mf, keep(fin.at[half]), part.at[k])

        @pl.when(lax.rem(k, 2) == 1)
        def _():
            q = lax.div(k, 2)
            rows = pair_rows(q)
            for i in range(32):
                res[i, rows, :] = jnp.concatenate([fin[0, i], fin[1, i]], 0).astype(BF16)
            out_copy(q).start()

    def early(k, _):
        first_own(k)
        return 0

    lax.fori_loop(0, EARLY, early, 0)
    pl.semaphore_wait(barrier, len(peers))
    each(PAIRS, lambda q: coeff_send(q).start())
    lax.fori_loop(EARLY, TILES, early, 0)

    stages = tuple(zip(LAGS, (first_level, second_own, second_level, regroup, third_level, fourth_own, fourth_level)))

    def step(n, _):
        for late, stage in stages:

            @pl.when(jnp.logical_and(n >= late, n < TILES + late))
            def _(late=late, stage=stage):
                stage(n - late)

        return 0

    lax.fori_loop(0, TILES + stages[-1][0], step, 0)

    def finish(k):
        far_send(k).wait_send()
        for d in (1, 2, 3):
            y_send(k, d).wait_send()
        last_send(k).wait_send()

        @pl.when(k > 0)
        def _():
            swap_send(k).wait_send()

    def finish_pair(q):
        coeff_send(q).wait_send()
        out_copy(q).wait()

    each(TILES, finish)
    each(PAIRS, finish_pair)


def per_device(coeffs, source_mats, middle_mats, target_mats):
    hbm = pl.BlockSpec(memory_space=pl.ANY)
    vm = lambda *s: pltpu.VMEM(s, BF16)
    dma = lambda *s: pltpu.SemaphoreType.DMA(s)
    out = pl.pallas_call(
        kernel,
        out_shape=jax.ShapeDtypeStruct((32, 64, 128), BF16),
        in_specs=[hbm] * 4,
        out_specs=hbm,
        scratch_shapes=[
            vm(2, 2, 32, 32, 1024),
            vm(32, 32, 1024),
            vm(2, 2, 32, 32, 1024),
            vm(2, 32, 64, 128),
            vm(8, *TILE),
            vm(8, *TILE),
            vm(8, *TILE),
            vm(8, *TILE),
            vm(8, 2, 2, 4, 16, 128),
            vm(8, 4, 2, 4, 16, 128),
            vm(8, *TILE),
            vm(8, *TILE),
            vm(32, 64, 128),
            pltpu.VMEM((2, 32, 8, 128), F32),
            pltpu.VMEM((2, 2, 4, 32, 128), F32),
            pltpu.VMEM((8, 32, 8, 128), F32),
            pltpu.VMEM((2, 32, 8, 128), F32),
            dma(9, 4), dma(4), dma(4), dma(4), dma(8), dma(8), dma(8), dma(8),
            pltpu.SemaphoreType.DMA,
            dma(8, 4), dma(8, 4), dma(8), dma(8), dma(8), dma(4),
        ],
        compiler_params=pltpu.CompilerParams(
            collective_id=0, has_side_effects=True, vmem_limit_bytes=60 << 20
        ),
        name="butterfly",
    )(
        coeffs.reshape(32, 8, 8, 128).swapaxes(1, 2).reshape(32, 64, 128),
        source_mats,
        middle_mats,
        target_mats,
    )
    return out.reshape(32, 8, 8, 128).swapaxes(1, 2).reshape(32, 8, 1024)


def solution(mesh):
    return jax.shard_map(
        per_device,
        mesh=mesh,
        in_specs=(
            P(None, None, ("outer", "inner")),
            P(None, None, None, None, ("outer", "inner")),
            P(None, None, ("outer", "inner")),
            P(None, None, None, None, ("outer", "inner")),
        ),
        out_specs=P(None, None, ("outer", "inner")),
        check_vma=False,
    )
```

```python
import jax
import jax.numpy as jnp
from jax import lax
from jax.experimental import pallas as pl
from jax.experimental.pallas import tpu as pltpu
from jax.sharding import PartitionSpec as P

F32 = jnp.float32
BF16 = jnp.bfloat16
MESH = pl.DeviceIdType.MESH
TILES = 8
EARLY = 4
LAGS = (0, 0, 3, 5, 7, 8, 9)
PAIRS = 4
TILE = (16, 16, 128)


def flip1(v):
    return v + 1 - 2 * lax.rem(v, 2)


def flip(v, k):
    total = 0
    for bit in (1, 2, 4):
        total = total + bit * lax.rem(lax.div(v, bit) + lax.div(k, bit), 2)
    return total


def lane_blocks(v):
    lane = lax.broadcasted_iota(jnp.int32, (16, 128), 1)
    low = lane < 64
    even = (lane & 32) == 0
    s = [None] * 4
    for a in range(2):
        s[a] = jnp.where(low, v[a], pltpu.roll(v[a + 2], 64, 1))
        s[a + 2] = jnp.where(low, pltpu.roll(v[a], 64, 1), v[a + 2])
    out = [None] * 4
    for a in (0, 2):
        out[a] = jnp.where(even, s[a], pltpu.roll(s[a + 1], 32, 1))
        out[a + 1] = jnp.where(even, pltpu.roll(s[a], 96, 1), s[a + 1])
    return out


def level(mats, xf, mf, emit, part=None, halfway=None):
    n = len(mats)

    def widen(g, slot):
        for s in range(n):
            mf[slot, s] = mats[s](g * 4).astype(F32)

    widen(0, 0)

    def body(h, _):
        for slot in range(2):
            g = h * 2 + slot
            widen(lax.rem(g + 1, 8), 1 - slot)
            acc = [None if part is None else part[g * 4 + i] for i in range(4)]
            for s in range(n):
                for j in range(32):
                    x = xf[s, j]
                    for i in range(4):
                        v = x * mf[slot, s, i, j : j + 1, :]
                        acc[i] = v if acc[i] is None else acc[i] + v
            emit(g * 4, acc)
        if halfway is not None:
            pl.when(h == 1)(halfway)
        return 0

    lax.fori_loop(0, 4, body, 0)


def kernel(
    coeffs, source, middle, target, out,
    ms, mm, mt, c0, x1, x1p, snd, rcv, pk, un, x4, x4p, res, xf, mf, part, fin,
    m_sem, c_sem, cs_sem, cr_sem, xs_sem, xr_sem, as_sem, ar_sem, al_sem,
    ys_sem, yr_sem, yl_sem, ts_sem, tr_sem, o_sem,
):
    outer, inner = lax.axis_index("outer"), lax.axis_index("inner")
    own, y = lax.div(inner, 4), lax.rem(inner, 4)
    core_dev = (flip1(outer), inner)
    far_dev = (lax.rem(outer + 2, 4), inner)

    def ring_dev(k):
        return (outer, flip(own, k) * 4 + y)

    def y_dev(d):
        return (outer, own * 4 + flip(y, d))

    def tile(k):
        return flip(own, k)

    def lanes(k):
        return pl.ds(pl.multiple_of(tile(k) * 128, 128), 128)

    def pair(q):
        return flip(lax.div(own, 2), q)

    def pair_lanes(q):
        return pl.ds(pl.multiple_of(pair(q) * 256, 256), 256)

    def pair_rows(q):
        return pl.ds(pl.multiple_of(pair(q) * 16, 16), 16)

    def mat_copy(stage, q):
        r = pair_lanes(q)
        if stage < 4:
            at = (stage // 2, stage % 2, slice(None), slice(None), r)
            ends = (source.at[at], ms.at[at])
        elif stage == 4:
            ends = (middle.at[:, :, r], mm.at[:, :, r])
        else:
            at = ((stage - 5) // 2, (stage - 5) % 2, slice(None), slice(None), r)
            ends = (target.at[at], mt.at[at])
        return pltpu.make_async_copy(*ends, m_sem.at[stage, q])

    def coeff_copy(q):
        return pltpu.make_async_copy(coeffs.at[:, pair_rows(q)], c0.at[0, :, pair_rows(q)], c_sem.at[q])

    def remote(src, dst, send, recv, device):
        return pltpu.make_async_remote_copy(
            src_ref=src, dst_ref=dst, send_sem=send, recv_sem=recv, device_id=device, device_id_type=MESH
        )

    def coeff_send(q):
        return remote(coeffs.at[:, pair_rows(q)], c0.at[1, :, pair_rows(q)], cs_sem.at[q], cr_sem.at[q], core_dev)

    def part_of(k, u):
        return (k, pl.ds(u * 8, 8))

    def far_send(k, u):
        at = part_of(k, u)
        return remote(x1.at[at], x1p.at[at], xs_sem.at[k, u], xr_sem.at[k, u], far_dev)

    def swap_send(k, u):
        at = part_of(k, u)
        return remote(snd.at[at], rcv.at[at], as_sem.at[k, u], ar_sem.at[k, u], ring_dev(k))

    def swap_local():
        return pltpu.make_async_copy(snd.at[0], rcv.at[0], al_sem)

    def y_send(k, d):
        return remote(
            pk.at[k, lax.div(flip(y, d), 2)], un.at[k, y], ys_sem.at[k, d], yr_sem.at[k, d], y_dev(d)
        )

    def y_arrival(k, d):
        return remote(
            pk.at[k, lax.div(flip(y, d), 2)], un.at[k, flip(y, d)], ys_sem.at[k, d], yr_sem.at[k, d], y_dev(d)
        )

    def y_local(k):
        return pltpu.make_async_copy(pk.at[k, lax.div(y, 2)], un.at[k, y], yl_sem.at[k])

    def last_send(k, u):
        at = part_of(k, u)
        return remote(x4.at[at], x4p.at[at], ts_sem.at[k, u], tr_sem.at[k, u], y_dev(2))

    def out_copy(q):
        return pltpu.make_async_copy(res.at[:, pair_rows(q)], out.at[:, pair_rows(q)], o_sem.at[q])

    def each(count, fn):
        def body(k, _):
            fn(k)
            return 0

        lax.fori_loop(0, count, body, 0)

    barrier = pltpu.get_barrier_semaphore()
    peers = [core_dev, far_dev] + [y_dev(d) for d in (1, 2, 3)] + [ring_dev(k) for k in range(1, 8)]
    for peer in peers:
        pl.semaphore_signal(barrier, inc=1, device_id=peer, device_id_type=MESH)

    def start_pair(q):
        coeff_copy(q).start()
        mat_copy(0, q).start()

    each(PAIRS, start_pair)
    for stage in range(1, 9):
        each(PAIRS, lambda q, stage=stage: mat_copy(stage, q).start())

    def await_pair(k, *waits):
        @pl.when(lax.rem(k, 2) == 0)
        def _():
            for wait in waits:
                wait(lax.div(k, 2))

    def mats(ref, lead, k):
        ln = lanes(k)
        return [lambda i, at=at: ref[(*at, pl.ds(i, 4), slice(None), ln)] for at in lead]

    def fill(s, ref):
        for h in range(16):
            v = ref[h].astype(F32)
            xf[s, 2 * h] = v[:8]
            xf[s, 2 * h + 1] = v[8:]

    def emit_to(ref):
        def emit(i, acc):
            h = lax.div(i, 2)
            for a in range(2):
                ref[h + a] = jnp.concatenate(acc[2 * a : 2 * a + 2], 0).astype(BF16)

        return emit

    def keep(ref):
        def emit(i, acc):
            for a in range(4):
                ref[i + a] = acc[a]

        return emit

    def first_fill(s, k):
        upper = lax.rem(tile(k), 2) == 1
        rows = pair_rows(lax.div(k, 2))
        for j in range(32):
            v = c0[s, j, rows, :].astype(F32)
            xf[0, j] = jnp.where(upper, v[8:], v[:8])

    def first_own(k):
        await_pair(k, lambda q: coeff_copy(q).wait(), lambda q: mat_copy(0, q).wait())
        first_fill(0, k)
        level(mats(ms, ((0, 0),), k), xf, mf, keep(part.at[k]))

    def first_level(k):
        await_pair(k, lambda q: coeff_send(q).wait_recv(), lambda q: mat_copy(1, q).wait())
        first_fill(1, k)
        level(mats(ms, ((0, 1),), k), xf, mf, emit_to(x1.at[k]), part.at[k], lambda: far_send(k, 0).start())
        far_send(k, 1).start()

    def second_own(k):
        await_pair(k, lambda q: mat_copy(2, q).wait())
        fill(0, x1.at[k])
        level(mats(ms, ((1, 0),), k), xf, mf, keep(part.at[k]))

    def second_level(k):
        await_pair(k, lambda q: mat_copy(3, q).wait(), lambda q: mat_copy(4, q).wait())
        far_send(k, 0).wait_recv()
        far_send(k, 1).wait_recv()
        fill(0, x1p.at[k])

        def emit(i, acc):
            for a in range(4):
                xf[1, i + a] = acc[a].astype(BF16).astype(F32)

        level(mats(ms, ((1, 1),), k), xf, mf, emit, part.at[k])
        def halfway():
            @pl.when(k > 0)
            def _():
                swap_send(k, 0).start()

        level(mats(mm, ((),), k), xf.at[1:2], mf, emit_to(snd.at[k]), None, halfway)

        @pl.when(k == 0)
        def _():
            swap_local().start()

        @pl.when(k > 0)
        def _():
            swap_send(k, 1).start()

    def regroup(k):
        @pl.when(k == 0)
        def _():
            swap_local().wait()

        @pl.when(k > 0)
        def _():
            swap_send(k, 0).wait_recv()
            swap_send(k, 1).wait_recv()

        for a in range(4):
            v = lane_blocks([rcv[k, a * 4 + c].astype(F32) for c in range(4)])
            for b in range(4):
                pk[k, b // 2, b % 2, a] = v[b].astype(BF16)
        for d in (1, 2, 3):
            y_send(k, d).start()
        y_local(k).start()

    def third_level(k):
        await_pair(k, lambda q: mat_copy(5, q).wait(), lambda q: mat_copy(6, q).wait())
        y_local(k).wait()
        for d in (1, 2, 3):
            y_arrival(k, d).wait_recv()
        for s in range(2):
            which = lax.rem(y, 2) if s == 0 else 1 - lax.rem(y, 2)
            for a in range(4):
                v = lane_blocks([un[k, b, which, a].astype(F32) for b in range(4)])
                for c in range(4):
                    xf[s, a * 8 + c * 2] = v[c][:8]
                    xf[s, a * 8 + c * 2 + 1] = v[c][8:]
        level(mats(mt, ((0, 0), (0, 1)), k), xf, mf, emit_to(x4.at[k]), None, lambda: last_send(k, 0).start())
        last_send(k, 1).start()

    def fourth_own(k):
        await_pair(k, lambda q: mat_copy(7, q).wait())
        fill(0, x4.at[k])
        level(mats(mt, ((1, 0),), k), xf, mf, keep(part.at[k]))

    def fourth_level(k):
        await_pair(k, lambda q: mat_copy(8, q).wait())
        last_send(k, 0).wait_recv()
        last_send(k, 1).wait_recv()
        fill(0, x4p.at[k])
        half = lax.rem(tile(k), 2)
        level(mats(mt, ((1, 1),), k), xf, mf, keep(fin.at[half]), part.at[k])

        @pl.when(lax.rem(k, 2) == 1)
        def _():
            q = lax.div(k, 2)
            rows = pair_rows(q)
            for i in range(32):
                res[i, rows, :] = jnp.concatenate([fin[0, i], fin[1, i]], 0).astype(BF16)
            out_copy(q).start()

    def early(k, _):
        first_own(k)
        return 0

    lax.fori_loop(0, EARLY, early, 0)
    pl.semaphore_wait(barrier, len(peers))
    each(PAIRS, lambda q: coeff_send(q).start())
    lax.fori_loop(EARLY, TILES, early, 0)

    stages = tuple(zip(LAGS, (first_level, second_own, second_level, regroup, third_level, fourth_own, fourth_level)))

    def step(n, _):
        for late, stage in stages:
            joined = late > LAGS[2]

            @pl.when(jnp.logical_and(n >= late, n < TILES + late - joined))
            def _(late=late, stage=stage, joined=joined):
                def run(k, _):
                    stage(k)
                    return 0

                k = n - late
                lax.fori_loop(k, jnp.where(k == 6, 8, k + 1) if joined else k + 1, run, 0)

        return 0

    lax.fori_loop(0, TILES + max(LAGS) - 1, step, 0)

    def finish(k):
        far_send(k, 0).wait_send()
        far_send(k, 1).wait_send()
        for d in (1, 2, 3):
            y_send(k, d).wait_send()
        last_send(k, 0).wait_send()
        last_send(k, 1).wait_send()

        @pl.when(k > 0)
        def _():
            swap_send(k, 0).wait_send()
            swap_send(k, 1).wait_send()

    def finish_pair(q):
        coeff_send(q).wait_send()
        out_copy(q).wait()

    each(TILES, finish)
    each(PAIRS, finish_pair)


def per_device(coeffs, source_mats, middle_mats, target_mats):
    hbm = pl.BlockSpec(memory_space=pl.ANY)
    vm = lambda *s: pltpu.VMEM(s, BF16)
    dma = lambda *s: pltpu.SemaphoreType.DMA(s)
    out = pl.pallas_call(
        kernel,
        out_shape=jax.ShapeDtypeStruct((32, 64, 128), BF16),
        in_specs=[hbm] * 4,
        out_specs=hbm,
        scratch_shapes=[
            vm(2, 2, 32, 32, 1024),
            vm(32, 32, 1024),
            vm(2, 2, 32, 32, 1024),
            vm(2, 32, 64, 128),
            vm(8, *TILE),
            vm(8, *TILE),
            vm(8, *TILE),
            vm(8, *TILE),
            vm(8, 2, 2, 4, 16, 128),
            vm(8, 4, 2, 4, 16, 128),
            vm(8, *TILE),
            vm(8, *TILE),
            vm(32, 64, 128),
            pltpu.VMEM((2, 32, 8, 128), F32),
            pltpu.VMEM((2, 2, 4, 32, 128), F32),
            pltpu.VMEM((8, 32, 8, 128), F32),
            pltpu.VMEM((2, 32, 8, 128), F32),
            dma(9, 4), dma(4), dma(4), dma(4), dma(8, 2), dma(8, 2), dma(8, 2), dma(8, 2),
            pltpu.SemaphoreType.DMA,
            dma(8, 4), dma(8, 4), dma(8), dma(8, 2), dma(8, 2), dma(4),
        ],
        compiler_params=pltpu.CompilerParams(
            collective_id=0, has_side_effects=True, vmem_limit_bytes=60 << 20
        ),
        name="butterfly",
    )(
        coeffs.reshape(32, 8, 8, 128).swapaxes(1, 2).reshape(32, 64, 128),
        source_mats,
        middle_mats,
        target_mats,
    )
    return out.reshape(32, 8, 8, 128).swapaxes(1, 2).reshape(32, 8, 1024)


def solution(mesh):
    return jax.shard_map(
        per_device,
        mesh=mesh,
        in_specs=(
            P(None, None, ("outer", "inner")),
            P(None, None, None, None, ("outer", "inner")),
            P(None, None, ("outer", "inner")),
            P(None, None, None, None, ("outer", "inner")),
        ),
        out_specs=P(None, None, ("outer", "inner")),
        check_vma=False,
    )
```
